256 devices in a mesh: dp: 16 (over x, y), expert: 16 (over z, core).
Axes of the slice: x: 4, y: 4, z: 8, core: 2. Of those that a mesh axis runs over, the one named last changes fastest.
Arguments:
- tokens: bfloat16 [32768, 7168], P(('dp', 'expert')), may hold values from -6 to 6
- tangent: bfloat16 [32768, 7168], P(('dp', 'expert')), may hold values from -6 to 6
- expert_ids: int32 [32768, 8], P(('dp', 'expert')), may hold values from 0 to 255, as said below
- gates: bfloat16 [32768, 8], P(('dp', 'expert')), may hold values from 0.049804688 to 0.5
- precision: float32 [7168], replicated, may hold values from 1 to 10
- gate_weight: bfloat16 [16, 1792, 2048], P('expert', None, 'dp'), may hold values from -0.0625 to 0.0625
- up_weight: bfloat16 [16, 1792, 2048], P('expert', None, 'dp'), may hold values from -0.0625 to 0.0625
- down_weight: bfloat16 [16, 1792, 2048], P('expert', None, 'dp'), may hold values from -0.125 to 0.125
Outputs:
- grad_gate: bfloat16 [16, 1792, 2048], P('expert', None, 'dp')
- grad_up: bfloat16 [16, 1792, 2048], P('expert', None, 'dp')
- grad_down: bfloat16 [16, 1792, 2048], P('expert', None, 'dp')
The draws below stay inside these ranges and needn't reach their ends.
Inputs may be any that keep to these rules, and one draw needn't show every extreme that they name: `expert_ids`: each row names 8 different experts. The rows of one device name each expert below 4 at least once and at most 4 times, and in every draw the rows of every device name one such expert exactly 4 times.
All inputs are finite; a program needn't handle non-finite values.
Results may differ from the reference program's by a relative error of at most 0.024.
Values may be sent and summed in bfloat16 or wider, within the bound.
No kernel may reach another device: no remote copies, remote signals or barrier semaphores. Data moves between devices by JAX's collectives and lax.ppermute only.
A program may use at most 128 MiB of HBM per device.

```python
import math
import jax
import jax.numpy as jnp
from jax import lax

D = 7168
FF = 2048
ROUTED = 256
TOP = 8
EXPERTS = 4
CAP = 4
TOK_DEV = 128
REPLICAS = 4
HIDDEN_DEV = 128
TOKENS = 32768
N_DP = 16
N_EXPERT = 16


def draw_expert_ids(key, part):
    key = jax.random.fold_in(key, 11)
    blocks = N_DP * N_EXPERT
    key_count, key_busy, key_pick, key_fill, key_shuffle = jax.random.split(key, 5)
    counts = jax.random.randint(key_count, (blocks, EXPERTS), 1, CAP + 1)
    busiest = jax.random.randint(key_busy, (), 0, EXPERTS)
    counts = jnp.where(jnp.arange(EXPERTS)[None, :] == busiest, CAP, counts)
    scores = jax.random.randint(key_pick, (blocks, EXPERTS, TOK_DEV), 0, 1 << 16) * TOK_DEV + jnp.arange(TOK_DEV)[None, None, :]
    ranking = jnp.argsort(jnp.argsort(scores, axis=2), axis=2)
    chosen = ranking < counts[:, :, None]
    forced = jnp.transpose(chosen, (0, 2, 1)).reshape(blocks * TOK_DEV, EXPERTS)
    baseline = jax.random.randint(key_fill, (blocks * TOK_DEV, ROUTED), 0, 1 << 16) * ROUTED + jnp.arange(ROUTED)[None, :]
    window = jnp.concatenate([jnp.where(forced, (1 << 26) + baseline[:, :EXPERTS], -1), baseline[:, EXPERTS:]], axis=1)
    _, picked_ids = lax.top_k(window, TOP)
    ordering = jax.random.randint(key_shuffle, (blocks * TOK_DEV, TOP), 0, 1 << 16) * TOP + jnp.arange(TOP)[None, :]
    shuffle = jnp.argsort(ordering, axis=1)
    picked_ids = jnp.take_along_axis(picked_ids, shuffle, axis=1)
    return picked_ids.astype(jnp.int32)


def shard_levels(own_key, shape, cuts, smallest, high):
    def one(dim, shards_of):
        heights = jax.random.uniform(jax.random.fold_in(jax.random.fold_in(own_key, 6), dim), (shards_of,), jnp.float32, smallest / len(cuts), high / len(cuts))
        return jnp.repeat(jnp.exp(heights), shape[dim] // shards_of).reshape((-1,) + (1,) * (len(shape) - dim - 1))

    loudness = one(*cuts[0])
    for cut in cuts[1:]:
        loudness = loudness * one(*cut)
    return loudness


def centred(stream_key, extent, spread, bound, cuts=(), held_as=jnp.bfloat16):
    drawn = jax.random.normal(stream_key, extent, jnp.float32) * spread
    if len(cuts) > 0:
        drawn = shard_levels(stream_key, extent, cuts, -0.22, 0.18) * drawn
    return jnp.clip(drawn, min=-bound, max=bound).astype(held_as)


def setup_inputs(seed: int = 0) -> dict:
    keys = jax.random.split(jax.random.key(seed), 9)
    tokens = centred(keys[0], (TOKENS, D), 1.0, 6.0, ((0, 256),))
    tangent = centred(keys[1], (TOKENS, D), 1.0, 6.0, ((0, 256),))
    expert_ids = draw_expert_ids(jax.random.fold_in(keys[8], 71), 0)
    gates = jnp.clip(jnp.exp(math.log(0.5) - 2.306499 * jax.random.uniform(keys[3], (TOKENS, TOP), jnp.float32) ** shard_levels(keys[3], (TOKENS, TOP), ((0, 256),), -0.2, 0.2)), 0.049804688, 0.5).astype(jnp.bfloat16)
    precision = jnp.clip(jnp.exp(jax.random.uniform(keys[4], (D,), jnp.float32, math.log(1.0), math.log(10.0))), 1.0, 10.0)
    gate_weight = centred(keys[5], (N_EXPERT, D // REPLICAS, FF), D ** -0.5, 0.0625, ((0, 16), (2, 16)))
    up_weight = centred(keys[6], (N_EXPERT, D // REPLICAS, FF), D ** -0.5, 0.0625, ((0, 16), (2, 16)))
    down_weight = centred(keys[7], (N_EXPERT, D // REPLICAS, FF), FF ** -0.5, 0.125, ((0, 16), (2, 16)))
    return {"tokens": tokens, "tangent": tangent, "expert_ids": expert_ids, "gates": gates, "precision": precision, "gate_weight": gate_weight, "up_weight": up_weight, "down_weight": down_weight}


def silu_parts(preact):
    sigma_val = jax.nn.sigmoid(preact)
    return preact * sigma_val, sigma_val * (1.0 + preact * (1.0 - sigma_val))


def reference(tokens, tangent, expert_ids, gates, precision, gate_weight, up_weight, down_weight):
    blocks = N_DP * N_EXPERT
    replicas = N_EXPERT // EXPERTS
    flat_ids = expert_ids.reshape(blocks, TOK_DEV * TOP)
    onehot = (flat_ids[:, :, None] == jnp.arange(EXPERTS, dtype=jnp.int32)[None, None, :]).astype(jnp.int32)
    before = jnp.cumsum(onehot, axis=1) - onehot
    slot_of = jnp.sum(before * onehot, axis=2).reshape(blocks, TOK_DEV, TOP).astype(jnp.int32)
    inside = jnp.sum(onehot, axis=2).reshape(blocks, TOK_DEV, TOP).astype(jnp.int32)
    owner_of = jnp.where(inside > 0, expert_ids.reshape(blocks, TOK_DEV, TOP), EXPERTS).astype(jnp.int32)
    safe_owner = jnp.minimum(owner_of, EXPERTS - 1).astype(jnp.int32)
    block_index = jnp.broadcast_to(jnp.arange(blocks, dtype=jnp.int32)[:, None, None], owner_of.shape)
    gate_values = gates.reshape(blocks, TOK_DEV, TOP, 1).astype(jnp.float32) * inside[:, :, :, None].astype(jnp.float32)

    def place_rows(values):
        buffer = jnp.zeros((EXPERTS, blocks, CAP, D), jnp.bfloat16)
        buffer = buffer.at[owner_of, block_index, slot_of].set(values, mode="drop")
        return buffer.reshape(EXPERTS, blocks * CAP, D)

    def spread_rows(source):
        return jnp.broadcast_to(source.reshape(blocks, TOK_DEV, 1, D), (blocks, TOK_DEV, TOP, D))

    gate_full = gate_weight.reshape(EXPERTS, D, FF)
    up_full = up_weight.reshape(EXPERTS, D, FF)
    down_full = down_weight.reshape(EXPERTS, D, FF)
    routed_x = place_rows(spread_rows(tokens))
    routed_dx = place_rows(spread_rows(tangent))

    def pre_acts(x_rows, dx_rows, w_gate, w_up):
        gate_pre = jnp.dot(x_rows, w_gate, preferred_element_type=jnp.float32)
        up_pre = jnp.dot(x_rows, w_up, preferred_element_type=jnp.float32)
        gate_tan = jnp.dot(dx_rows, w_gate, preferred_element_type=jnp.float32)
        up_tan = jnp.dot(dx_rows, w_up, preferred_element_type=jnp.float32)
        return gate_pre, up_pre, gate_tan, up_tan

    def forward(inputs):
        x_rows, dx_rows, w_gate, w_up, w_down = inputs
        gate_pre, up_pre, gate_tan, up_tan = pre_acts(x_rows, dx_rows, w_gate, w_up)
        activated, derivative = silu_parts(gate_pre)
        hidden_tan = (derivative * gate_tan * up_pre + activated * up_tan).astype(jnp.bfloat16)
        slice_sums = jnp.einsum("rsh,dsh->srd", hidden_tan.reshape(-1, N_DP, HIDDEN_DEV).astype(jnp.float32),
                                w_down.reshape(D, N_DP, HIDDEN_DEV).astype(jnp.float32),
                                precision=lax.Precision.HIGHEST)
        slice_sums = lax.optimization_barrier(slice_sums.astype(jnp.bfloat16))
        return jnp.sum(slice_sums.astype(jnp.float32), axis=0).astype(jnp.bfloat16)

    returned = lax.map(forward, (routed_x, routed_dx, gate_full, up_full, down_full))
    returned = returned.reshape(EXPERTS, blocks, CAP, D)
    picked = returned[safe_owner, block_index, slot_of]
    combined = jnp.sum(gate_values * picked.astype(jnp.float32), axis=2).reshape(TOKENS, D)
    cotangent = (precision[None, :] * combined).astype(jnp.bfloat16)
    cot_routes = (gate_values * cotangent.reshape(blocks, TOK_DEV, 1, D).astype(jnp.float32)).astype(jnp.bfloat16)
    routed_cot = place_rows(cot_routes)

    def backward(inputs):
        x_rows, dx_rows, c_rows, w_gate, w_up, w_down = inputs
        gate_pre, up_pre, gate_tan, up_tan = pre_acts(x_rows, dx_rows, w_gate, w_up)
        activated, derivative = silu_parts(gate_pre)
        hidden_out = (activated * up_pre).astype(jnp.bfloat16)
        back_grad = jnp.dot(c_rows, w_down, preferred_element_type=jnp.float32)
        grad_down = jnp.dot(c_rows.T, hidden_out, preferred_element_type=jnp.float32).astype(jnp.bfloat16)
        gate_cot = (back_grad * up_pre * derivative).astype(jnp.bfloat16)
        up_cot = (back_grad * activated).astype(jnp.bfloat16)
        grad_gate = jnp.dot(x_rows.T, gate_cot, preferred_element_type=jnp.float32).astype(jnp.bfloat16)
        grad_up = jnp.dot(x_rows.T, up_cot, preferred_element_type=jnp.float32).astype(jnp.bfloat16)
        return grad_gate, grad_up, grad_down

    grad_gate, grad_up, grad_down = lax.map(backward, (routed_x, routed_dx, routed_cot, gate_full, up_full, down_full))
    shape_out = (N_EXPERT, D // replicas, FF)
    return (grad_gate.reshape(shape_out), grad_up.reshape(shape_out), grad_down.reshape(shape_out))
```

```python
import jax
import jax.numpy as jnp
from jax import lax
from jax.sharding import Mesh, PartitionSpec as P

EXPERTS = 4
CAP = 4
NX, NY, NZ, NC = 4, 4, 8, 2
RING = 4
BF16 = jnp.bfloat16
F32 = jnp.float32
ALL = ("x", "y", "z", "c")


def sigmoid_parts(preact):
    sigma_val = jax.nn.sigmoid(preact)
    return preact * sigma_val, sigma_val * (1.0 + preact * (1.0 - sigma_val))


def plane_shift(value, step, first):
    pairs = []
    for x in range(NX):
        for y in range(NY):
            for c in range(NC):
                if (c == 0) == first:
                    to = ((x + step) % NX, y, c)
                else:
                    to = (x, (y + step) % NY, c)
                pairs.append(((x * NY + y) * NC + c, (to[0] * NY + to[1]) * NC + to[2]))
    return lax.ppermute(value, ("x", "y", "c"), pairs)


def gather_phase(value, first):
    return [value] + [plane_shift(value, step, first) for step in (1, 2, 3)]


def plane_gather(value):
    got = lax.optimization_barrier(tuple(gather_phase(value, True)))
    return gather_phase(jnp.stack(got), False)


def scatter_phase(pieces, first):
    moved = [pieces[0]] + [plane_shift(pieces[step], -step, first) for step in (1, 2, 3)]
    moved = lax.optimization_barrier(tuple(moved))
    total = moved[0].astype(F32)
    for piece in moved[1:]:
        total = total + piece.astype(F32)
    return total.astype(BF16)


def core_swap(value):
    return lax.ppermute(value, "c", [(0, 1), (1, 0)])


def z_swap(value):
    return lax.ppermute(value, "z", [(z, z ^ 1) for z in range(NZ)])


def core_sum(value):
    other = core_swap(value)
    return value + jnp.swapaxes(other, 0, 1)


def body(tokens, tangent, expert_ids, gates, precision, gate_weight, up_weight, down_weight):
    tok_rows, features = tokens.shape
    block = gate_weight.shape[1]
    hidden = gate_weight.shape[2]
    half = 2 * block
    core = lax.axis_index("c")
    parity = lax.axis_index("z") % 2

    onehot = expert_ids[:, :, None] == jnp.arange(EXPERTS, dtype=jnp.int32)[None, None, :]
    has = jnp.any(onehot, axis=1)
    gate = jnp.sum(jnp.where(onehot, gates[:, :, None], jnp.zeros((), BF16)), axis=1)
    order = jnp.arange(tok_rows, dtype=jnp.int32)
    earlier = (order[None, :] < order[:, None]).astype(BF16)
    before = jnp.dot(earlier, has.astype(BF16), preferred_element_type=F32)
    slots = jnp.arange(CAP, dtype=F32)
    hit = has[:, :, None] & (before[:, :, None] == slots[None, None, :])
    selector = hit.astype(BF16).reshape(tok_rows, EXPERTS * CAP)
    placed = jnp.where(hit, gate[:, :, None], jnp.zeros((), BF16)).reshape(tok_rows, EXPERTS * CAP)

    both = jnp.stack([tokens, tangent])
    chosen = jnp.einsum("tr,ktd->krd", selector, both, preferred_element_type=F32).astype(BF16)
    chosen = chosen.reshape(2, NZ, 2, 2, NC, block)
    chosen = jnp.transpose(chosen, (1, 4, 0, 2, 3, 5)).reshape(NZ * NC * 4, half)
    sent = lax.all_to_all(chosen, ("z", "c"), 0, 0, tiled=True)
    rows = jnp.transpose(sent.reshape(NZ * NC, 2, 2, half), (1, 0, 2, 3)).reshape(2, 2 * NZ * NC, half)
    per = 2 * NZ * NC

    wg, wu, wd, rows = lax.optimization_barrier((gate_weight[0], up_weight[0], down_weight[0], rows))

    def join(own):
        other = z_swap(own)
        return jnp.where(
            parity == 0, jnp.concatenate([own, other], 0), jnp.concatenate([other, own], 0)
        )

    weight_in = jnp.concatenate([join(wg), join(wu)], axis=1)
    weight_down = join(wd)

    shared = lax.dot_general(
        selector, placed, (((0,), (0,)), ((), ())), preferred_element_type=F32
    ).astype(BF16)
    shared_other = core_swap(shared)
    pair = jnp.stack(
        [jnp.where(core == 0, shared, shared_other), jnp.where(core == 0, shared_other, shared)]
    ).reshape(NC, NZ, 2, NZ, 2)
    eye = jnp.eye(NC, dtype=BF16)
    mixing = pair[:, :, :, None, :, :] * eye[:, None, None, :, None, None]
    mixing = jnp.transpose(mixing, (1, 0, 2, 4, 3, 5)).reshape(per, per)
    row_gate = jnp.sum(jnp.where(jnp.eye(per, dtype=jnp.bool_), mixing, jnp.zeros((), BF16)), axis=1)
    row_gate = row_gate.astype(F32)
    prec = jnp.where(
        core == 0,
        precision.reshape(2, NC, block)[:, 0].reshape(1, half),
        precision.reshape(2, NC, block)[:, 1].reshape(1, half),
    )

    pieces = plane_gather(rows)
    pre = [
        jnp.dot(
            piece.reshape(RING * 2 * per, half), weight_in, preferred_element_type=F32
        ).reshape(RING, 2, per, 2 * hidden)
        for piece in pieces
    ]
    pre = core_sum(jnp.stack(pre))
    gate_pre, up_pre = pre[:, :, 0, :, :hidden], pre[:, :, 0, :, hidden:]
    gate_tan, up_tan = pre[:, :, 1, :, :hidden], pre[:, :, 1, :, hidden:]
    activated, derivative = sigmoid_parts(gate_pre)
    hidden_tan = (derivative * gate_tan * up_pre + activated * up_tan).astype(BF16)
    hidden_out = (activated * up_pre).astype(BF16)

    product = [
        lax.dot_general(
            hidden_tan[j].reshape(RING * per, hidden),
            weight_down,
            (((1,), (1,)), ((), ())),
            preferred_element_type=F32,
        ).astype(BF16).reshape(RING, per, half)
        for j in range(RING)
    ]
    summed = scatter_phase(product, False)
    summed = scatter_phase([summed[i] for i in range(RING)], True)

    x_rows = jnp.stack([piece[:, 0] for piece in pieces]).reshape(RING * RING * per, half)
    x_own = jnp.where(parity == 0, x_rows[:, :block], x_rows[:, block:])
    x_give = jnp.where(parity == 0, x_rows[:, block:], x_rows[:, :block])
    x_other = z_swap(x_give)

    returned = lax.all_to_all(summed, "z", 0, 0, tiled=True)
    combined = jnp.dot(mixing, returned, preferred_element_type=F32)
    cotangent = (prec * combined).astype(BF16)
    cot_rows = (row_gate[:, None] * cotangent.astype(F32)).astype(BF16)
    cot_sent = lax.all_to_all(cot_rows, "z", 0, 0, tiled=True)
    cot_pieces = plane_gather(cot_sent)
    back = [
        jnp.dot(
            piece.reshape(RING * per, half), weight_down, preferred_element_type=F32
        ).reshape(RING, per, hidden)
        for piece in cot_pieces
    ]
    back = core_sum(jnp.stack(back))
    gate_cot = (back * up_pre * derivative).astype(BF16)
    up_cot = (back * activated).astype(BF16)
    cots = jnp.concatenate([gate_cot, up_cot], axis=-1).reshape(RING * RING * per, 2 * hidden)
    cots_other = z_swap(cots)

    contract = (((0,), (0,)), ((), ()))
    c_rows = jnp.stack(cot_pieces).reshape(RING * RING * per, half)
    down_part = lax.dot_general(
        c_rows, hidden_out.reshape(RING * RING * per, hidden), contract, preferred_element_type=F32
    )
    down_own = jnp.where(parity == 0, down_part[:block], down_part[block:])
    down_give = jnp.where(parity == 0, down_part[block:], down_part[:block])
    down_other = z_swap(down_give.astype(BF16))
    grad_down = (down_own + down_other.astype(F32)).astype(BF16)

    grads = lax.dot_general(x_own, cots, contract, preferred_element_type=F32)
    grads = grads + lax.dot_general(x_other, cots_other, contract, preferred_element_type=F32)
    grad_gate = grads[:, :hidden].astype(BF16)
    grad_up = grads[:, hidden:].astype(BF16)
    return grad_gate[None], grad_up[None], grad_down[None]


def solution(mesh):
    fine = Mesh(mesh.devices.reshape(NX, NY, NZ, NC), ALL)
    rows = P(ALL, None)
    weights = P(("z", "c"), None, ("x", "y"))
    in_specs = (rows, rows, rows, rows, P(), weights, weights, weights)
    out_specs = (weights, weights, weights)
    return jax.shard_map(body, mesh=fine, in_specs=in_specs, out_specs=out_specs, check_vma=False)
```

```python
import jax
import jax.numpy as jnp
from jax import lax
from jax.sharding import Mesh, PartitionSpec as P

EXPERTS = 4
CAP = 4
NX, NY, NE, NP, NC = 4, 4, 4, 2, 2
RING = 4
BF16 = jnp.bfloat16
F32 = jnp.float32
ALL = ("x", "y", "e", "p", "c")


def sigmoid_parts(preact):
    sigma_val = jax.nn.sigmoid(preact)
    return preact * sigma_val, sigma_val * (1.0 + preact * (1.0 - sigma_val))


def fence(*values):
    return lax.optimization_barrier(values)


def plane_shift(value, step, first):
    pairs = []
    for x in range(NX):
        for y in range(NY):
            for c in range(NC):
                if (c == 0) == first:
                    to = ((x + step) % NX, y, c)
                else:
                    to = (x, (y + step) % NY, c)
                pairs.append(((x * NY + y) * NC + c, (to[0] * NY + to[1]) * NC + to[2]))
    return lax.ppermute(value, ("x", "y", "c"), pairs)


def gather_phase(value, first):
    return fence(value, *[plane_shift(value, step, first) for step in (1, 2, 3)])


def gather_pair(low, high, first):
    low, high = fence(low, high)
    low_1, high_3 = plane_shift(low, 1, first), plane_shift(high, -1, first)
    high_1, low_3 = plane_shift(high, 1, first), plane_shift(low, -1, first)
    low_2, high_2 = plane_shift(low_1, 1, first), plane_shift(high_3, -1, first)
    return (low, low_1, low_2, low_3), (high, high_1, high_2, high_3)


def scatter_phase(pieces, first):
    moved = [pieces[0]] + [plane_shift(pieces[step], -step, first) for step in (1, 2, 3)]
    moved = fence(*moved)
    total = moved[0].astype(F32)
    for piece in moved[1:]:
        total = total + piece.astype(F32)
    return total.astype(BF16)


def core_swap(value):
    return lax.ppermute(value, "c", [(0, 1), (1, 0)])


def pair_swap(value):
    return lax.ppermute(value, "p", [(0, 1), (1, 0)])


def expert_shift(value, step):
    return lax.ppermute(value, "e", [(e, (e + step) % NE) for e in range(NE)])


def expert_swap(pieces, sign):
    return fence(pieces[0], *[expert_shift(pieces[r], sign * r) for r in (1, 2, 3)])


def body(tokens, tangent, expert_ids, gates, precision, gate_weight, up_weight, down_weight):
    tok_rows = tokens.shape[0]
    block = gate_weight.shape[1]
    hidden = gate_weight.shape[2]
    half = 2 * block
    core = lax.axis_index("c")
    parity = lax.axis_index("p")
    expert = lax.axis_index("e")
    per = NE * NC * CAP
    each = NC * CAP
    all_rows = RING * RING * per

    names = (expert + jnp.arange(EXPERTS, dtype=jnp.int32)) % EXPERTS
    onehot = expert_ids[:, :, None] == names[None, None, :]
    has = jnp.any(onehot, axis=1)
    gate = jnp.sum(jnp.where(onehot, gates[:, :, None], jnp.zeros((), BF16)), axis=1)
    order = jnp.arange(tok_rows, dtype=jnp.int32)
    earlier = (order[None, :] < order[:, None]).astype(BF16)
    before = jnp.dot(earlier, has.astype(BF16), preferred_element_type=F32)
    slots = jnp.arange(CAP, dtype=F32)
    hit = has[:, :, None] & (before[:, :, None] == slots[None, None, :])
    selector = hit.astype(BF16).reshape(tok_rows, EXPERTS * CAP)
    placed = jnp.where(hit, gate[:, :, None], jnp.zeros((), BF16)).reshape(tok_rows, EXPERTS * CAP)

    def pick(source):
        rows = lax.dot_general(
            selector, source, (((0,), (0,)), ((), ())), preferred_element_type=F32
        ).astype(BF16)
        return rows.reshape(EXPERTS, CAP, 2 * NC, block)

    def blocks_of(picked, to_core):
        own, other = 2 * parity + to_core, 2 * (1 - parity) + to_core
        return jnp.stack(
            [
                lax.dynamic_index_in_dim(rows, q, 2, False)
                for q in (own, other)
                for rows in picked
            ],
            axis=1,
        ).reshape(NE, 4 * CAP, block)

    picked = (pick(tokens), pick(tangent))
    mine = blocks_of(picked, core)
    theirs = core_swap(blocks_of(picked, 1 - core))
    chosen = jnp.concatenate(
        [jnp.where(core == 0, mine, theirs), jnp.where(core == 0, theirs, mine)], axis=1
    )
    sent = expert_swap([chosen[r] for r in range(NE)], 1)
    rows = jnp.stack(sent).reshape(NE, NC, 2, 2, CAP, block)
    rows = jnp.transpose(rows, (2, 3, 0, 1, 4, 5)).reshape(2, 2, per, block)

    wd = down_weight[0]
    in_own = jnp.concatenate([gate_weight[0], up_weight[0]], axis=1)
    in_own, wd, rows = fence(in_own, wd, rows)
    in_other = pair_swap(in_own)
    wd_other = pair_swap(wd)

    shared = lax.dot_general(
        selector, placed, (((0,), (0,)), ((), ())), preferred_element_type=F32
    ).astype(BF16)
    shared_other = core_swap(shared)
    rows, shared_other = fence(rows, shared_other)
    first = jnp.where(core == 0, shared, shared_other).reshape(NE, CAP, NE, CAP)
    second = jnp.where(core == 0, shared_other, shared).reshape(NE, CAP, NE, CAP)
    zero = jnp.zeros_like(first)
    mixing = jnp.stack(
        [jnp.stack([first, zero], axis=3), jnp.stack([zero, second], axis=3)], axis=1
    ).reshape(per, per)
    row_gate = jnp.sum(jnp.where(jnp.eye(per, dtype=jnp.bool_), mixing, jnp.zeros((), BF16)), axis=1)
    row_gate = row_gate.astype(F32)
    prec = precision.reshape(2 * NC, block)
    prec = jnp.concatenate(
        [
            lax.dynamic_index_in_dim(prec, 2 * parity + core, 0, True),
            lax.dynamic_index_in_dim(prec, 2 * (1 - parity) + core, 0, True),
        ],
        axis=1,
    )

    got = gather_phase(rows, True)
    low = jnp.stack([piece[0] for piece in got])
    high = jnp.stack([piece[1] for piece in got])
    low, high = gather_pair(low, high, False)
    pre = [
        jnp.dot(low[j].reshape(-1, block), in_own, preferred_element_type=F32)
        + jnp.dot(high[j].reshape(-1, block), in_other, preferred_element_type=F32)
        for j in range(RING)
    ]
    pre = jnp.stack(pre).reshape(RING, RING, 2, per, 2 * hidden)
    pre, wd_other = fence(pre, wd_other)
    pre_other = core_swap(pre.astype(BF16))
    x_give = jnp.concatenate([piece[:, 0].reshape(-1, block) for piece in high])
    pre_other, x_give = fence(pre_other, x_give)
    x_other = pair_swap(x_give)
    pre = pre + jnp.swapaxes(pre_other, 0, 1).astype(F32)
    gate_pre, up_pre = pre[:, :, 0, :, :hidden], pre[:, :, 0, :, hidden:]
    gate_tan, up_tan = pre[:, :, 1, :, :hidden], pre[:, :, 1, :, hidden:]
    activated, derivative = sigmoid_parts(gate_pre)
    hidden_tan = (derivative * gate_tan * up_pre + activated * up_tan).astype(BF16)
    (hidden_tan,) = fence(hidden_tan)
    hidden_out = (activated * up_pre).astype(BF16).reshape(all_rows, hidden)

    weight_down = jnp.concatenate([wd, wd_other], axis=0)
    product = [
        lax.dot_general(
            hidden_tan[j].reshape(RING * per, hidden),
            weight_down,
            (((1,), (1,)), ((), ())),
            preferred_element_type=F32,
        ).astype(BF16).reshape(RING, per, half)
        for j in range(RING)
    ]
    summed = scatter_phase(product, False)
    summed = scatter_phase([summed[i] for i in range(RING)], True)
    summed, x_other = fence(summed, x_other)
    returned = jnp.concatenate(expert_swap([summed[each * r : each * (r + 1)] for r in range(NE)], -1))
    combined = jnp.dot(mixing, returned, preferred_element_type=F32)
    cotangent = (prec * combined).astype(BF16)
    cot = (row_gate[:, None] * cotangent.astype(F32)).astype(BF16)
    cot = jnp.concatenate(expert_swap([cot[each * r : each * (r + 1)] for r in range(NE)], 1))
    cot = gather_phase(cot, True)
    c_other = jnp.stack([piece[:, block:] for piece in cot])
    c_own = jnp.stack([piece[:, :block] for piece in cot])
    c_other = [c_other] + [plane_shift(c_other, step, False) for step in (1, 3, 2)]
    c_own, c_other[1] = fence(c_own, c_other[1])
    c_own = [c_own] + [plane_shift(c_own, step, False) for step in (1, 3, 2)]
    c_other = [c_other[k] for k in (0, 1, 3, 2)]
    c_own = [c_own[k] for k in (0, 1, 3, 2)]
    c_other = jnp.concatenate([piece.reshape(-1, block) for piece in c_other])
    c_own = jnp.concatenate([piece.reshape(-1, block) for piece in c_own])

    contract = (((0,), (0,)), ((), ()))
    down_give = lax.dot_general(c_other, hidden_out, contract, preferred_element_type=F32)
    down_other = pair_swap(down_give.astype(BF16))
    back = jnp.dot(c_own, wd, preferred_element_type=F32)
    back = back + jnp.dot(c_other, wd_other, preferred_element_type=F32)
    back = back.reshape(RING, RING, per, hidden)
    back = back + jnp.swapaxes(core_swap(back), 0, 1)
    gate_cot = (back * up_pre * derivative).astype(BF16)
    up_cot = (back * activated).astype(BF16)
    cots = jnp.concatenate([gate_cot, up_cot], axis=-1).reshape(all_rows, 2 * hidden)
    cots_other = pair_swap(cots)

    down_own = lax.dot_general(c_own, hidden_out, contract, preferred_element_type=F32)
    grad_down = (down_own + down_other.astype(F32)).astype(BF16)
    x_own = jnp.concatenate([piece[:, 0].reshape(-1, block) for piece in low])

    grads = lax.dot_general(x_own, cots, contract, preferred_element_type=F32)
    grads = grads + lax.dot_general(x_other, cots_other, contract, preferred_element_type=F32)
    grad_gate = grads[:, :hidden].astype(BF16)
    grad_up = grads[:, hidden:].astype(BF16)
    return grad_gate[None], grad_up[None], grad_down[None]


def solution(mesh):
    fine = Mesh(mesh.devices.reshape(NX, NY, NE, NP, NC), ALL)
    rows = P(ALL, None)
    weights = P(("e", "p", "c"), None, ("x", "y"))
    in_specs = (rows, rows, rows, rows, P(), weights, weights, weights)
    out_specs = (weights, weights, weights)
    return jax.shard_map(body, mesh=fine, in_specs=in_specs, out_specs=out_specs, check_vma=False)
```

```python
import jax
import jax.numpy as jnp
from jax import lax
from jax.sharding import Mesh, PartitionSpec as P

EXPERTS = 4
CAP = 4
NX, NY, NE, NP, NC = 4, 4, 4, 2, 2
RING = 4
BF16 = jnp.bfloat16
F32 = jnp.float32
ALL = ("x", "y", "e", "p", "c")


def sigmoid_parts(preact):
    sigma_val = jax.nn.sigmoid(preact)
    return preact * sigma_val, sigma_val * (1.0 + preact * (1.0 - sigma_val))


def fence(*values):
    return lax.optimization_barrier(values)


def plane_shift(value, step, first):
    pairs = []
    for x in range(NX):
        for y in range(NY):
            for c in range(NC):
                if (c == 0) == first:
                    to = ((x + step) % NX, y, c)
                else:
                    to = (x, (y + step) % NY, c)
                pairs.append(((x * NY + y) * NC + c, (to[0] * NY + to[1]) * NC + to[2]))
    return lax.ppermute(value, ("x", "y", "c"), pairs)


def gather_phase(value, first):
    return fence(value, *[plane_shift(value, step, first) for step in (1, 2, 3)])


def gather_pair(low, high, first):
    low, high = fence(low, high)
    low_1, high_3 = plane_shift(low, 1, first), plane_shift(high, -1, first)
    high_1, low_3 = plane_shift(high, 1, first), plane_shift(low, -1, first)
    low_2, high_2 = plane_shift(low_1, 1, first), plane_shift(high_3, -1, first)
    return (low, low_1, low_2, low_3), (high, high_1, high_2, high_3)


def scatter_phase(pieces, first):
    moved = [pieces[0]] + [plane_shift(pieces[step], -step, first) for step in (1, 2, 3)]
    moved = fence(*moved)
    total = moved[0].astype(F32)
    for piece in moved[1:]:
        total = total + piece.astype(F32)
    return total.astype(BF16)


def scatter_ring(pieces, first):
    def plus(one, two):
        return (one.astype(F32) + two.astype(F32)).astype(BF16)

    low_2 = plane_shift(pieces[2][0], -1, first)
    high_2 = plane_shift(pieces[2][1], 1, first)
    high_1 = plane_shift(pieces[1][1], -1, first)
    low_3 = plane_shift(pieces[3][0], 1, first)
    low_2, high_2 = fence(low_2, high_2)
    low_1 = plane_shift(plus(pieces[1][0], low_2), -1, first)
    high_3 = plane_shift(plus(pieces[3][1], high_2), 1, first)
    low_1, high_3, high_1, low_3 = fence(low_1, high_3, high_1, low_3)
    low = pieces[0][0].astype(F32) + low_1.astype(F32) + low_3.astype(F32)
    high = pieces[0][1].astype(F32) + high_1.astype(F32) + high_3.astype(F32)
    return low.astype(BF16), high.astype(BF16)


def core_swap(value):
    return lax.ppermute(value, "c", [(0, 1), (1, 0)])


def pair_swap(value):
    return lax.ppermute(value, "p", [(0, 1), (1, 0)])


def expert_shift(value, step):
    return lax.ppermute(value, "e", [(e, (e + step) % NE) for e in range(NE)])


def expert_swap(pieces, sign):
    return fence(pieces[0], *[expert_shift(pieces[r], sign * r) for r in (1, 2, 3)])


def body(tokens, tangent, expert_ids, gates, precision, gate_weight, up_weight, down_weight):
    tok_rows = tokens.shape[0]
    block = gate_weight.shape[1]
    hidden = gate_weight.shape[2]
    half = 2 * block
    core = lax.axis_index("c")
    parity = lax.axis_index("p")
    expert = lax.axis_index("e")
    per = NE * NC * CAP
    each = NC * CAP
    all_rows = RING * RING * per

    names = (expert + jnp.arange(EXPERTS, dtype=jnp.int32)) % EXPERTS
    onehot = expert_ids[:, :, None] == names[None, None, :]
    has = jnp.any(onehot, axis=1)
    gate = jnp.sum(jnp.where(onehot, gates[:, :, None], jnp.zeros((), BF16)), axis=1)
    order = jnp.arange(tok_rows, dtype=jnp.int32)
    earlier = (order[None, :] < order[:, None]).astype(BF16)
    before = jnp.dot(earlier, has.astype(BF16), preferred_element_type=F32)
    slots = jnp.arange(CAP, dtype=F32)
    hit = has[:, :, None] & (before[:, :, None] == slots[None, None, :])
    selector = hit.astype(BF16).reshape(tok_rows, EXPERTS * CAP)
    placed = jnp.where(hit, gate[:, :, None], jnp.zeros((), BF16)).reshape(tok_rows, EXPERTS * CAP)

    def pick(source):
        rows = lax.dot_general(
            selector, source, (((0,), (0,)), ((), ())), preferred_element_type=F32
        ).astype(BF16)
        return rows.reshape(EXPERTS, CAP, 2 * NC, block)

    def blocks_of(picked, to_core):
        own, other = 2 * parity + to_core, 2 * (1 - parity) + to_core
        return jnp.stack(
            [
                lax.dynamic_index_in_dim(rows, q, 2, False)
                for q in (own, other)
                for rows in picked
            ],
            axis=1,
        ).reshape(NE, 4 * CAP, block)

    picked = (pick(tokens), pick(tangent))
    mine = blocks_of(picked, core)
    theirs = core_swap(blocks_of(picked, 1 - core))
    chosen = jnp.concatenate(
        [jnp.where(core == 0, mine, theirs), jnp.where(core == 0, theirs, mine)], axis=1
    )
    sent = expert_swap([chosen[r] for r in range(NE)], 1)
    rows = jnp.stack(sent).reshape(NE, NC, 2, 2, CAP, block)
    rows = jnp.transpose(rows, (2, 3, 0, 1, 4, 5)).reshape(2, 2, per, block)

    wd = down_weight[0]
    in_own = jnp.concatenate([gate_weight[0], up_weight[0]], axis=1)
    in_own, wd, rows = fence(in_own, wd, rows)
    in_other = pair_swap(in_own)
    wd_other = pair_swap(wd)

    shared = lax.dot_general(
        selector, placed, (((0,), (0,)), ((), ())), preferred_element_type=F32
    ).astype(BF16)
    shared_other = core_swap(shared)
    rows, shared_other = fence(rows, shared_other)
    first = jnp.where(core == 0, shared, shared_other).reshape(NE, CAP, NE, CAP)
    second = jnp.where(core == 0, shared_other, shared).reshape(NE, CAP, NE, CAP)
    zero = jnp.zeros_like(first)
    mixing = jnp.stack(
        [jnp.stack([first, zero], axis=3), jnp.stack([zero, second], axis=3)], axis=1
    ).reshape(per, per)
    row_gate = jnp.sum(jnp.where(jnp.eye(per, dtype=jnp.bool_), mixing, jnp.zeros((), BF16)), axis=1)
    row_gate = row_gate.astype(F32)
    prec = precision.reshape(2 * NC, block)
    prec = jnp.concatenate(
        [
            lax.dynamic_index_in_dim(prec, 2 * parity + core, 0, True),
            lax.dynamic_index_in_dim(prec, 2 * (1 - parity) + core, 0, True),
        ],
        axis=1,
    )

    got = gather_phase(rows, True)
    low = jnp.stack([piece[0] for piece in got])
    high = jnp.stack([piece[1] for piece in got])
    low, high = gather_pair(low, high, False)
    pre = [
        jnp.dot(low[j].reshape(-1, block), in_own, preferred_element_type=F32)
        + jnp.dot(high[j].reshape(-1, block), in_other, preferred_element_type=F32)
        for j in range(RING)
    ]
    pre = jnp.stack(pre).reshape(RING, RING, 2, per, 2 * hidden)
    pre, wd_other = fence(pre, wd_other)
    pre_other = core_swap(pre.astype(BF16))
    x_first = pair_swap(high[0][:, 0].reshape(-1, block))
    x_second = pair_swap(jnp.concatenate([piece[:, 0].reshape(-1, block) for piece in high[1:]]))
    pre = pre + jnp.swapaxes(pre_other, 0, 1).astype(F32)
    gate_pre, up_pre = pre[:, :, 0, :, :hidden], pre[:, :, 0, :, hidden:]
    gate_tan, up_tan = pre[:, :, 1, :, :hidden], pre[:, :, 1, :, hidden:]
    activated, derivative = sigmoid_parts(gate_pre)
    hidden_tan = (derivative * gate_tan * up_pre + activated * up_tan).astype(BF16)
    (hidden_tan,) = fence(hidden_tan)
    hidden_out = (activated * up_pre).astype(BF16).reshape(all_rows, hidden)

    weight_down = jnp.concatenate([wd, wd_other], axis=0)
    def product(j, n):
        rows = hidden_tan[j].reshape(2, RING // 2 * per, hidden)[n]
        value = lax.dot_general(
            rows, weight_down, (((1,), (1,)), ((), ())), preferred_element_type=F32
        )
        return value.astype(BF16).reshape(RING // 2, per, half)

    low_sum, high_sum = scatter_ring([[product(j, n) for n in (0, 1)] for j in range(RING)], False)
    low_sum, high_sum, x_first = fence(low_sum, high_sum, x_first)
    summed = [low_sum[0], low_sum[1], high_sum[0], high_sum[1]]
    summed = scatter_phase(summed, True)
    returned = jnp.concatenate(expert_swap([summed[each * r : each * (r + 1)] for r in range(NE)], -1))
    combined = jnp.dot(mixing, returned, preferred_element_type=F32)
    cotangent = (prec * combined).astype(BF16)
    cot = (row_gate[:, None] * cotangent.astype(F32)).astype(BF16)
    cot = jnp.concatenate(expert_swap([cot[each * r : each * (r + 1)] for r in range(NE)], 1))
    cot = gather_phase(cot, True)
    c_other = jnp.stack([piece[:, block:] for piece in cot])
    c_own = jnp.stack([piece[:, :block] for piece in cot])
    c_other = [c_other] + [plane_shift(c_other, step, False) for step in (1, 3, 2)]
    c_own, c_other[1] = fence(c_own, c_other[1])
    c_own = [c_own] + [plane_shift(c_own, step, False) for step in (1, 3, 2)]
    c_other = [c_other[k] for k in (0, 1, 3, 2)]
    c_own = [c_own[k] for k in (0, 1, 3, 2)]
    *c_other, x_second = fence(*c_other, x_second)
    c_other = jnp.concatenate([piece.reshape(-1, block) for piece in c_other])
    c_own = jnp.concatenate([piece.reshape(-1, block) for piece in c_own])

    contract = (((0,), (0,)), ((), ()))
    down_give = lax.dot_general(c_other, hidden_out, contract, preferred_element_type=F32)
    down_other = pair_swap(down_give.astype(BF16))
    back = jnp.dot(c_own, wd, preferred_element_type=F32)
    back = back + jnp.dot(c_other, wd_other, preferred_element_type=F32)
    back = back.reshape(RING, RING, per, hidden)
    back = back + jnp.swapaxes(core_swap(back), 0, 1)
    gate_cot = (back * up_pre * derivative).astype(BF16)
    up_cot = (back * activated).astype(BF16)
    cots = jnp.concatenate([gate_cot, up_cot], axis=-1).reshape(all_rows, 2 * hidden)
    cots_other = pair_swap(cots)

    down_own = lax.dot_general(c_own, hidden_out, contract, preferred_element_type=F32)
    grad_down = (down_own + down_other.astype(F32)).astype(BF16)
    x_own = jnp.concatenate([piece[:, 0].reshape(-1, block) for piece in low])

    grads = lax.dot_general(x_own, cots, contract, preferred_element_type=F32)
    x_other = jnp.concatenate([x_first, x_second])
    grads = grads + lax.dot_general(x_other, cots_other, contract, preferred_element_type=F32)
    grad_gate = grads[:, :hidden].astype(BF16)
    grad_up = grads[:, hidden:].astype(BF16)
    return grad_gate[None], grad_up[None], grad_down[None]


def solution(mesh):
    fine = Mesh(mesh.devices.reshape(NX, NY, NE, NP, NC), ALL)
    rows = P(ALL, None)
    weights = P(("e", "p", "c"), None, ("x", "y"))
    in_specs = (rows, rows, rows, rows, P(), weights, weights, weights)
    out_specs = (weights, weights, weights)
    return jax.shard_map(body, mesh=fine, in_specs=in_specs, out_specs=out_specs, check_vma=False)
```

```python
import jax
import jax.numpy as jnp
from jax import lax
from jax.sharding import Mesh, PartitionSpec as P

EXPERTS = 4
CAP = 4
NX, NY, NE, NP, NC = 4, 4, 4, 2, 2
RING = 4
BF16 = jnp.bfloat16
F32 = jnp.float32
ALL = ("x", "y", "e", "p", "c")


def sigmoid_parts(preact):
    sigma_val = jax.nn.sigmoid(preact)
    return preact * sigma_val, sigma_val * (1.0 + preact * (1.0 - sigma_val))


def fence(*values):
    return lax.optimization_barrier(values)


def plane_shift(value, step, first):
    pairs = []
    for x in range(NX):
        for y in range(NY):
            for c in range(NC):
                if (c == 0) == first:
                    to = ((x + step) % NX, y, c)
                else:
                    to = (x, (y + step) % NY, c)
                pairs.append(((x * NY + y) * NC + c, (to[0] * NY + to[1]) * NC + to[2]))
    return lax.ppermute(value, ("x", "y", "c"), pairs)


def gather_phase(value, first):
    return fence(value, *[plane_shift(value, step, first) for step in (1, 2, 3)])


def gather_pair(low, high, first):
    low, high = fence(low, high)
    low_1, high_3 = plane_shift(low, 1, first), plane_shift(high, -1, first)
    high_1, low_3 = plane_shift(high, 1, first), plane_shift(low, -1, first)
    low_2, high_2 = plane_shift(low_1, 1, first), plane_shift(high_3, -1, first)
    return (low, low_1, low_2, low_3), (high, high_1, high_2, high_3)


def scatter_phase(pieces, first):
    moved = [pieces[0]] + [plane_shift(pieces[step], -step, first) for step in (1, 2, 3)]
    moved = fence(*moved)
    total = moved[0].astype(F32)
    for piece in moved[1:]:
        total = total + piece.astype(F32)
    return total.astype(BF16)


def scatter_ring(pieces, first):
    def plus(one, two):
        return (one.astype(F32) + two.astype(F32)).astype(BF16)

    low_2 = plane_shift(pieces[2][0], -1, first)
    high_2 = plane_shift(pieces[2][1], 1, first)
    high_1 = plane_shift(pieces[1][1], -1, first)
    low_3 = plane_shift(pieces[3][0], 1, first)
    low_2, high_2 = fence(low_2, high_2)
    low_1 = plane_shift(plus(pieces[1][0], low_2), -1, first)
    high_3 = plane_shift(plus(pieces[3][1], high_2), 1, first)
    low_1, high_3, high_1, low_3 = fence(low_1, high_3, high_1, low_3)
    low = pieces[0][0].astype(F32) + low_1.astype(F32) + low_3.astype(F32)
    high = pieces[0][1].astype(F32) + high_1.astype(F32) + high_3.astype(F32)
    return low.astype(BF16), high.astype(BF16)


def core_swap(value):
    return lax.ppermute(value, "c", [(0, 1), (1, 0)])


def pair_swap(value):
    return lax.ppermute(value, "p", [(0, 1), (1, 0)])


def expert_shift(value, step):
    return lax.ppermute(value, "e", [(e, (e + step) % NE) for e in range(NE)])


def expert_swap(pieces, sign):
    return fence(pieces[0], *[expert_shift(pieces[r], sign * r) for r in (1, 2, 3)])


def body(tokens, tangent, expert_ids, gates, precision, gate_weight, up_weight, down_weight):
    tok_rows = tokens.shape[0]
    block = gate_weight.shape[1]
    hidden = gate_weight.shape[2]
    half = 2 * block
    core = lax.axis_index("c")
    parity = lax.axis_index("p")
    expert = lax.axis_index("e")
    per = NE * NC * CAP
    each = NC * CAP
    all_rows = RING * RING * per

    names = (expert + jnp.arange(EXPERTS, dtype=jnp.int32)) % EXPERTS
    onehot = expert_ids[:, :, None] == names[None, None, :]
    has = jnp.any(onehot, axis=1)
    gate = jnp.sum(jnp.where(onehot, gates[:, :, None], jnp.zeros((), BF16)), axis=1)
    order = jnp.arange(tok_rows, dtype=jnp.int32)
    earlier = (order[None, :] < order[:, None]).astype(BF16)
    before = jnp.dot(earlier, has.astype(BF16), preferred_element_type=F32)
    slots = jnp.arange(CAP, dtype=F32)
    hit = has[:, :, None] & (before[:, :, None] == slots[None, None, :])
    selector = hit.astype(BF16).reshape(tok_rows, EXPERTS * CAP)
    placed = jnp.where(hit, gate[:, :, None], jnp.zeros((), BF16)).reshape(tok_rows, EXPERTS * CAP)

    def pick(source):
        rows = lax.dot_general(
            selector, source, (((0,), (0,)), ((), ())), preferred_element_type=F32
        ).astype(BF16)
        return rows.reshape(EXPERTS, CAP, 2 * NC, block)

    def blocks_of(picked, to_core):
        own, other = 2 * parity + to_core, 2 * (1 - parity) + to_core
        return jnp.stack(
            [
                lax.dynamic_index_in_dim(rows, q, 2, False)
                for q in (own, other)
                for rows in picked
            ],
            axis=1,
        ).reshape(NE, 4 * CAP, block)

    picked = (pick(tokens), pick(tangent))
    mine = blocks_of(picked, core)
    theirs = core_swap(blocks_of(picked, 1 - core))
    chosen = jnp.concatenate(
        [jnp.where(core == 0, mine, theirs), jnp.where(core == 0, theirs, mine)], axis=1
    )
    sent = expert_swap([chosen[r] for r in range(NE)], 1)
    rows = jnp.stack(sent).reshape(NE, NC, 2, 2, CAP, block)
    rows = jnp.transpose(rows, (2, 3, 0, 1, 4, 5)).reshape(2, 2, per, block)

    wd = down_weight[0]
    in_own = jnp.concatenate([gate_weight[0], up_weight[0]], axis=1)
    in_own, wd, rows = fence(in_own, wd, rows)
    in_other = pair_swap(in_own)
    wd_other = pair_swap(wd)

    shared = lax.dot_general(
        selector, placed, (((0,), (0,)), ((), ())), preferred_element_type=F32
    ).astype(BF16)
    shared_other = core_swap(shared)
    rows, shared_other = fence(rows, shared_other)
    first = jnp.where(core == 0, shared, shared_other).reshape(NE, CAP, NE, CAP)
    second = jnp.where(core == 0, shared_other, shared).reshape(NE, CAP, NE, CAP)
    zero = jnp.zeros_like(first)
    mixing = jnp.stack(
        [jnp.stack([first, zero], axis=3), jnp.stack([zero, second], axis=3)], axis=1
    ).reshape(per, per)
    row_gate = jnp.sum(jnp.where(jnp.eye(per, dtype=jnp.bool_), mixing, jnp.zeros((), BF16)), axis=1)
    row_gate = row_gate.astype(F32)
    prec = precision.reshape(2 * NC, block)
    prec = jnp.concatenate(
        [
            lax.dynamic_index_in_dim(prec, 2 * parity + core, 0, True),
            lax.dynamic_index_in_dim(prec, 2 * (1 - parity) + core, 0, True),
        ],
        axis=1,
    )

    got = gather_phase(rows, True)
    low = jnp.stack([piece[0] for piece in got])
    high = jnp.stack([piece[1] for piece in got])
    low, high = gather_pair(low, high, False)
    pre = [
        jnp.dot(low[j].reshape(-1, block), in_own, preferred_element_type=F32)
        + jnp.dot(high[j].reshape(-1, block), in_other, preferred_element_type=F32)
        for j in range(RING)
    ]
    pre = jnp.stack(pre).reshape(RING, RING, 2, per, 2 * hidden)
    pre, wd_other = fence(pre, wd_other)
    pre_other = core_swap(pre.astype(BF16))
    x_first = pair_swap(high[0][:, 0].reshape(-1, block))
    x_second = pair_swap(jnp.concatenate([piece[:, 0].reshape(-1, block) for piece in high[1:]]))
    pre = pre + jnp.swapaxes(pre_other, 0, 1).astype(F32)
    gate_pre, up_pre = pre[:, :, 0, :, :hidden], pre[:, :, 0, :, hidden:]
    gate_tan, up_tan = pre[:, :, 1, :, :hidden], pre[:, :, 1, :, hidden:]
    activated, derivative = sigmoid_parts(gate_pre)
    hidden_tan = (derivative * gate_tan * up_pre + activated * up_tan).astype(BF16)
    (hidden_tan,) = fence(hidden_tan)
    hidden_out = (activated * up_pre).astype(BF16).reshape(all_rows, hidden)

    weight_down = jnp.concatenate([wd, wd_other], axis=0)
    def product(j, n):
        rows = hidden_tan[j].reshape(2, RING // 2 * per, hidden)[n]
        value = lax.dot_general(
            rows, weight_down, (((1,), (1,)), ((), ())), preferred_element_type=F32
        )
        return value.astype(BF16).reshape(RING // 2, per, half)

    low_sum, high_sum = scatter_ring([[product(j, n) for n in (0, 1)] for j in range(RING)], False)
    low_sum, high_sum, x_first = fence(low_sum, high_sum, x_first)
    summed = [low_sum[0], low_sum[1], high_sum[0], high_sum[1]]
    summed = scatter_phase(summed, True)
    returned = jnp.concatenate(expert_swap([summed[each * r : each * (r + 1)] for r in range(NE)], -1))
    combined = jnp.dot(mixing, returned, preferred_element_type=F32)
    cotangent = (prec * combined).astype(BF16)
    cot = (row_gate[:, None] * cotangent.astype(F32)).astype(BF16)
    cot = jnp.concatenate(expert_swap([cot[each * r : each * (r + 1)] for r in range(NE)], 1))
    cot = gather_phase(cot, True)
    c_other = jnp.stack([piece[:, block:] for piece in cot])
    c_own = jnp.stack([piece[:, :block] for piece in cot])
    c_other = [c_other] + [plane_shift(c_other, step, False) for step in (1, 3, 2)]
    c_last, c_other[1] = fence(c_own, c_other[1])
    c_own = [c_own, plane_shift(c_own, 1, False), plane_shift(c_own, 3, False), plane_shift(c_last, 2, False)]
    c_other = [c_other[k] for k in (0, 1, 3, 2)]
    c_own = [c_own[k] for k in (0, 1, 3, 2)]
    *c_other, x_second = fence(*c_other, x_second)
    c_other = jnp.concatenate([piece.reshape(-1, block) for piece in c_other])
    c_own = jnp.concatenate([piece.reshape(-1, block) for piece in c_own])

    contract = (((0,), (0,)), ((), ()))
    down_give = lax.dot_general(c_other, hidden_out, contract, preferred_element_type=F32)
    down_other = pair_swap(down_give.astype(BF16))
    back = jnp.dot(c_own, wd, preferred_element_type=F32)
    back = back + jnp.dot(c_other, wd_other, preferred_element_type=F32)
    back = back.reshape(RING, RING, per, hidden)
    back = back + jnp.swapaxes(core_swap(back), 0, 1)
    gate_cot = (back * up_pre * derivative).astype(BF16)
    up_cot = (back * activated).astype(BF16)
    cots = jnp.concatenate([gate_cot, up_cot], axis=-1).reshape(all_rows, 2 * hidden)
    cots_other = pair_swap(cots)

    down_own = lax.dot_general(c_own, hidden_out, contract, preferred_element_type=F32)
    grad_down = (down_own + down_other.astype(F32)).astype(BF16)
    x_own = jnp.concatenate([piece[:, 0].reshape(-1, block) for piece in low])

    grads = lax.dot_general(x_own, cots, contract, preferred_element_type=F32)
    x_other = jnp.concatenate([x_first, x_second])
    grads = grads + lax.dot_general(x_other, cots_other, contract, preferred_element_type=F32)
    grad_gate = grads[:, :hidden].astype(BF16)
    grad_up = grads[:, hidden:].astype(BF16)
    return grad_gate[None], grad_up[None], grad_down[None]


def solution(mesh):
    fine = Mesh(mesh.devices.reshape(NX, NY, NE, NP, NC), ALL)
    rows = P(ALL, None)
    weights = P(("e", "p", "c"), None, ("x", "y"))
    in_specs = (rows, rows, rows, rows, P(), weights, weights, weights)
    out_specs = (weights, weights, weights)
    return jax.shard_map(body, mesh=fine, in_specs=in_specs, out_specs=out_specs, check_vma=False)
```
